32 devices in a mesh: fsdp: 4 (over z), ctx: 4 (over y, x), tp: 2 (over core).
Axes of the slice: x: 2, y: 2, z: 4, core: 2. Of those that a mesh axis runs over, the one named last changes fastest.
Arguments:
- layer_input: bfloat16 [8, 512, 768], P('fsdp', 'ctx'), may hold values from -6 to 6
- lengths: int32 [8], P('fsdp'), may hold values from 1 to 512, as said below
- first_gain: float32 [768], replicated, may hold values from 0.1 to 1.9
- first_shift: float32 [768], replicated, may hold values from -3 to 3
- qkv_weight: bfloat16 [3, 768, 768], P(None, ('fsdp', 'ctx'), 'tp'), may hold values from -0.3125 to 0.3125
- qv_bias: float32 [2, 768], P(None, 'tp'), may hold values from -3 to 3
- out_weight: bfloat16 [768, 768], P('tp', ('fsdp', 'ctx')), may hold values from -0.875 to 0.875
- out_bias: float32 [768], replicated, may hold values from -3 to 3
- second_gain: float32 [768], replicated, may hold values from 0.1 to 1.9
- second_shift: float32 [768], replicated, may hold values from -3 to 3
- up_weight: bfloat16 [768, 3072], P(('fsdp', 'ctx'), 'tp'), may hold values from -0.21875 to 0.21875
- up_bias: float32 [3072], P('tp'), may hold values from -3 to 3
- down_weight: bfloat16 [3072, 768], P('tp', ('fsdp', 'ctx')), may hold values from -0.109375 to 0.109375
- down_bias: float32 [768], replicated, may hold values from -3 to 3
- cotangent: bfloat16 [8, 512, 768], P('fsdp', 'ctx'), may hold values from -8 to 8
Outputs:
- layer_output: bfloat16 [8, 512, 768], P('fsdp', 'ctx')
- grad_input: float32 [8, 512, 768], P('fsdp', 'ctx')
- grad_firstgain: float32 [768], replicated
- grad_firstshift: float32 [768], replicated
- grad_qkvweight: float32 [3, 768, 768], P(None, ('fsdp', 'ctx'), 'tp')
- grad_qvbias: float32 [2, 768], P(None, 'tp')
- grad_outweight: float32 [768, 768], P('tp', ('fsdp', 'ctx'))
- grad_outbias: float32 [768], replicated
- grad_secondgain: float32 [768], replicated
- grad_secondshift: float32 [768], replicated
- grad_upweight: float32 [768, 3072], P(('fsdp', 'ctx'), 'tp')
- grad_upbias: float32 [3072], P('tp')
- grad_downweight: float32 [3072, 768], P('tp', ('fsdp', 'ctx'))
- grad_downbias: float32 [768], replicated
The draws below stay inside these ranges and needn't reach their ends.
Inputs may be any that keep to these rules, and one draw needn't show every extreme that they name: `lengths`: in the 2 sequences of each index of fsdp, one, chosen at random, has exactly 512 valid positions.
All inputs are finite; a program needn't handle non-finite values.
Results may differ from the reference program's by a relative error of at most 0.01.
The reference program's roundings to bfloat16 on the way count: a program that leaves them out, or rounds other values in their place, can miss the bound.
Values may be sent and summed in bfloat16 or wider, within the bound.
A program may use at most 128 MiB of HBM per device.

```python
import math
import jax
import jax.numpy as jnp
from jax import lax

D = 768
FF = 3072
HEAD = 64
LEN = 512
SEQS = 2
SEQUENCES = 8


def draw_lengths(key, part):
    key = jax.random.fold_in(key, 11)
    first_key, second_key = jax.random.split(key)
    groups = SEQUENCES // SEQS
    ragged = jax.random.randint(first_key, (groups, SEQS), 1, LEN + 1)
    chosen = jax.random.randint(second_key, (groups, 1), 0, SEQS)
    full_slot = jnp.arange(SEQS)[None, :] == chosen
    return jnp.where(full_slot, LEN, ragged).reshape(SEQUENCES).astype(jnp.int32)


def spiked(array, stream_key, source, target, parts, factor):
    def block_of(dim):
        return (jnp.arange(array.shape[dim]) // (array.shape[dim] // parts)).reshape((-1,) + (1,) * (array.ndim - 1 - dim))

    one_side = jax.random.permutation(stream_key, parts)[block_of(target)]
    second = (block_of(target) + parts // 2) % parts
    return jnp.where((block_of(source) == one_side) | (block_of(source) == second), factor * array, array)


def levels(key, shape, cuts, least, largest):
    loudness = 1.0
    for axis_at, parts in cuts:
        steps = jax.random.uniform(jax.random.fold_in(jax.random.fold_in(key, 6), axis_at), (parts,), jnp.float32, least / len(cuts), largest / len(cuts))
        loudness = loudness * jnp.repeat(jnp.exp(steps), shape[axis_at] // parts).reshape((-1,) + (1,) * (len(shape) - 1 - axis_at))
    return loudness


def noise(own_key, dims, width, limit, cuts=(), dtype=jnp.bfloat16):
    gain = levels(own_key, dims, cuts, -0.22, 0.18) if cuts else 1.0
    values = jax.random.normal(own_key, dims, jnp.float32) * width * gain
    return jnp.minimum(jnp.maximum(values, -limit), limit).astype(dtype)


def gaussian_with(own_key, shape, scale, limit, cuts, heavy, dtype=jnp.bfloat16):
    values = scale * jax.random.normal(own_key, shape, jnp.float32)
    if cuts:
        values = values * levels(own_key, shape, cuts, -0.22, 0.18)
    return jnp.clip(spiked(values, jax.random.fold_in(own_key, 3), *heavy), -limit, limit).astype(dtype)


def setup_inputs(seed: int = 0) -> dict:
    arg_keys = jax.random.split(jax.random.key(seed), 16)
    return {
        "layer_input": noise(arg_keys[0], (SEQUENCES, LEN, D), 1.0, 6.0, ((0, 4), (1, 4))),
        "lengths": draw_lengths(jax.random.fold_in(arg_keys[15], 71), 0),
        "first_gain": jnp.clip(1.0 + 0.18 * jax.random.normal(arg_keys[2], (D,), jnp.float32), 0.1, 1.9),
        "first_shift": noise(arg_keys[3], (D,), 0.5, 3.0, (), jnp.float32),
        "qkv_weight": noise(arg_keys[4], (3, D, D), (D // 2) ** -0.5, 0.3125, ((1, 16), (2, 2))),
        "qv_bias": noise(arg_keys[5], (2, D), 0.5, 3.0, ((1, 2),), jnp.float32),
        "out_weight": noise(arg_keys[6], (D, D), (D // 16) ** -0.5, 0.875, ((0, 2), (1, 16))),
        "out_bias": noise(arg_keys[7], (D,), 0.5, 3.0, (), jnp.float32),
        "second_gain": jnp.clip(1.0 + 0.18 * jax.random.normal(arg_keys[8], (D,), jnp.float32), 0.1, 1.9),
        "second_shift": noise(arg_keys[9], (D,), 0.5, 3.0, (), jnp.float32),
        "up_weight": noise(arg_keys[10], (D, FF), D ** -0.5, 0.21875, ((0, 16), (1, 2))),
        "up_bias": noise(arg_keys[11], (FF,), 0.5, 3.0, ((0, 2),), jnp.float32),
        "down_weight": noise(arg_keys[12], (FF, D), FF ** -0.5, 0.109375, ((0, 2), (1, 16))),
        "down_bias": noise(arg_keys[13], (D,), 0.5, 3.0, (), jnp.float32),
        "cotangent": gaussian_with(arg_keys[14], (SEQUENCES, LEN, D), 1.0, 8.0, ((0, 4), (1, 4)), (0, 2, 4, 2.0)),
    }


@jax.custom_vjp
def low(v):
    return lax.optimization_barrier(v.astype(jnp.bfloat16)).astype(jnp.float32)

@jax.custom_vjp
def low_back(v):
    return v

def low_keep(v):
    return (low(v), None)

def low_pass(kept, grad):
    return (grad,)

def back_keep(v):
    return (v, None)

def back_low(kept, grad):
    return (low(grad),)
low.defvjp(low_keep, low_pass)
low_back.defvjp(back_keep, back_low)

def norm_rows(rows_in, row_gain, row_shift):
    centre_mean = lax.optimization_barrier(jnp.mean(rows_in, axis=-1, keepdims=True))
    centred = rows_in - centre_mean
    variance = lax.optimization_barrier(jnp.mean(centred * centred, axis=-1, keepdims=True))
    return centred * lax.rsqrt(variance + 1e-05) * row_gain + row_shift

def matmul(left, right):
    return jnp.einsum('bld,de->ble', left, right, precision=lax.Precision.HIGHEST)

def decoder_layer(params, inputs, seq_lengths):
    first_gain, first_shift, qkv_weight, qv_bias, out_weight, out_bias, second_gain, second_shift, up_weight, up_bias, down_weight, down_bias = params
    batch_size = inputs.shape[0]
    head_shape = (batch_size, LEN, D // HEAD, HEAD)
    score_scale = 1.0 / math.sqrt(HEAD)
    normed = low(norm_rows(inputs, first_gain, first_shift))
    queries = low(low_back(matmul(normed, qkv_weight[0]) + qv_bias[0]))
    key_rows = low(low_back(matmul(normed, qkv_weight[1])))
    value_rows = low(low_back(matmul(normed, qkv_weight[2]) + qv_bias[1]))
    scores = jnp.einsum('bqhe,bkhe->bhqk', queries.reshape(head_shape), key_rows.reshape(head_shape), precision=lax.Precision.HIGHEST) * score_scale
    scores = low_back(scores)
    positions = jnp.arange(LEN)
    allowed = (positions[None, :] <= positions[:, None])[None, None] & (positions[None, None, None, :] < seq_lengths[:, None, None, None])
    probs = low(jax.nn.softmax(jnp.where(allowed, scores, -1e+30), axis=-1))
    attended = jnp.einsum('bhqk,bkhe->bqhe', probs, value_rows.reshape(head_shape), precision=lax.Precision.HIGHEST).reshape(batch_size, LEN, D)
    attended = low(low_back(attended))
    residual = inputs + low_back(matmul(attended, out_weight) + out_bias)
    normed_two = low(norm_rows(residual, second_gain, second_shift))
    up_proj = low_back(matmul(normed_two, up_weight) + up_bias)
    activated = low(jax.nn.gelu(up_proj, approximate=True))
    return residual + low_back(matmul(activated, down_weight) + down_bias)

def reference(layer_input, lengths, first_gain, first_shift, qkv_weight, qv_bias, out_weight, out_bias, second_gain, second_shift, up_weight, up_bias, down_weight, down_bias, cotangent):
    params = tuple((entry.astype(jnp.float32) for entry in (first_gain, first_shift, qkv_weight, qv_bias, out_weight, out_bias, second_gain, second_shift, up_weight, up_bias, down_weight, down_bias)))
    per_step = math.gcd(SEQUENCES, max(1, 4096 // LEN))
    scan_steps = SEQUENCES // per_step
    inputs = layer_input.astype(jnp.float32).reshape(scan_steps, per_step, LEN, D)
    cotangents = cotangent.astype(jnp.float32).reshape(scan_steps, per_step, LEN, D)
    length_steps = lengths.reshape(scan_steps, per_step)

    def accumulate(totals, entries):
        rows_now, lengths_now, cot_now = entries
        result, backward = jax.vjp(lambda p, r: decoder_layer(p, r, lengths_now), params, rows_now)
        gradients, grad_rows = backward(cot_now)
        totals = jax.tree.map(lambda a, b: a + b, totals, gradients)
        return (totals, (result.astype(jnp.bfloat16), grad_rows))
    zeroed = jax.tree.map(jnp.zeros_like, params)
    totals, (outputs, grad_rows) = lax.scan(accumulate, zeroed, (inputs, length_steps, cotangents))
    return (outputs.reshape(SEQUENCES, LEN, D), grad_rows.reshape(SEQUENCES, LEN, D), totals[0], totals[1], totals[2], totals[3], totals[4], totals[5], totals[6], totals[7], totals[8], totals[9], totals[10], totals[11])
```

```python
import functools
import math

import jax
import jax.numpy as jnp
from jax import lax
from jax.experimental import pallas as pl
from jax.experimental.pallas import tpu as pltpu
from jax.sharding import PartitionSpec as P

HEAD = 64
MESH = pl.DeviceIdType.MESH


def partners(z_peers):
    me_c = lax.axis_index("ctx")
    side = me_c + 1 - 2 * (me_c % 2)
    over = (me_c + 2) % 4
    me_f = lax.axis_index("fsdp")
    count = lax.axis_size("fsdp")
    peers = [(me_f + t) % count for t in range(1, count)] if z_peers else []
    return me_c, side, over, 3 - me_c, me_f, peers


def greet(side, over, peers):
    barrier = pltpu.get_barrier_semaphore()
    for target in (side, over):
        pl.semaphore_signal(barrier, inc=1, device_id={"ctx": target}, device_id_type=MESH)
    for target in peers:
        pl.semaphore_signal(barrier, inc=1, device_id={"fsdp": target}, device_id_type=MESH)
    pl.semaphore_wait(barrier, 2 + len(peers))


def remote(src, dst, send, recv, axis, target):
    return pltpu.make_async_remote_copy(
        src_ref=src, dst_ref=dst, send_sem=send, recv_sem=recv,
        device_id={axis: target}, device_id_type=MESH,
    )


def gather_kernel(arrays, slots, z_peers, *refs):
    ins, outs = refs[:arrays], refs[arrays : 2 * arrays]
    z_send, z_recv, xy_send, xy_recv = refs[2 * arrays :]
    me_c, side, over, _, me_f, peers = partners(z_peers)
    greet(side, over, peers)
    started = []

    def go(copy):
        copy.start()
        started.append(copy)

    def slot(s):
        return (me_f + s) % slots if z_peers else s

    def own(k, s):
        if z_peers and s > 0:
            return outs[k].at[slot(s), me_c]
        return ins[k].at[0 if z_peers else s]

    nearest = sorted(range(slots), key=lambda s: min(s, slots - s))
    if z_peers:
        for k in range(arrays):
            for t in nearest[1:]:
                go(remote(ins[k].at[0], outs[k].at[me_f, me_c], z_send.at[k, t], z_recv.at[k, slots - t], "fsdp", peers[t - 1]))
        order = [(k, 0) for k in range(arrays)]
        order += [(k, s) for k in range(arrays) for s in nearest[1:]]
    else:
        order = [(k, s) for k in range(arrays) for s in range(slots)]

    def forward(k, s):
        src = own(k, s)
        if z_peers and s > 0:
            remote(src, src, z_send.at[k, s], z_recv.at[k, s], "fsdp", peers[0]).wait_recv()
        dst = outs[k].at[slot(s), me_c]
        go(remote(src, dst, xy_send.at[0, k, s], xy_recv.at[0, k, s], "ctx", side))
        go(remote(src, dst, xy_send.at[1, k, s], xy_recv.at[1, k, s], "ctx", over))

    def arrived(way, k, s, from_c):
        ref = outs[k].at[slot(s), from_c]
        remote(ref, ref, xy_send.at[way, k, s], xy_recv.at[way, k, s], "ctx", side).wait_recv()
        return ref

    def relay(k, s):
        if (k + s) % 2 == 0:
            ref = arrived(0, k, s, side)
            go(remote(ref, ref, xy_send.at[2, k, s], xy_recv.at[2, k, s], "ctx", over))
        else:
            ref = arrived(1, k, s, over)
            go(remote(ref, ref, xy_send.at[2, k, s], xy_recv.at[2, k, s], "ctx", side))

    lag = 2 if len(order) > 4 else len(order)
    for at, (k, s) in enumerate(order):
        forward(k, s)
        if at >= lag:
            relay(*order[at - lag])
    for k in range(arrays):
        if z_peers:
            outs[k][me_f, me_c] = ins[k][0]
        else:
            for s in range(slots):
                outs[k][s, me_c] = ins[k][s]
    for k, s in order[len(order) - lag :]:
        relay(k, s)
    for k, s in order:
        if (k + s) % 2 == 0:
            arrived(1, k, s, over)
        else:
            arrived(0, k, s, side)
        arrived(2, k, s, 3 - me_c)
    for copy in started:
        copy.wait_send()


def gather_blocks(shards, slots, z_peers, collective_id):
    arrays = len(shards)
    spec = pl.BlockSpec(memory_space=pltpu.VMEM)
    size = sum(x.size * 2 for x in shards) * 4 * (slots if z_peers else 1)
    return pl.pallas_call(
        functools.partial(gather_kernel, arrays, slots, z_peers),
        out_shape=[jax.ShapeDtypeStruct((slots, 4) + x.shape[1:], x.dtype) for x in shards],
        in_specs=[spec] * arrays,
        out_specs=[spec] * arrays,
        scratch_shapes=[
            pltpu.SemaphoreType.DMA((arrays, slots)),
            pltpu.SemaphoreType.DMA((arrays, slots)),
            pltpu.SemaphoreType.DMA((3, arrays, slots)),
            pltpu.SemaphoreType.DMA((3, arrays, slots)),
        ],
        compiler_params=pltpu.CompilerParams(
            collective_id=collective_id, has_side_effects=True, vmem_limit_bytes=int(size * 1.25) + (4 << 20)
        ),
        cost_estimate=pl.CostEstimate(flops=0, bytes_accessed=2 * size, transcendentals=0),
    )(*shards)


def scatter_kernel(arrays, slots, z_peers, *refs):
    ins, outs = refs[:arrays], refs[arrays : 2 * arrays]
    per = refs[2 * arrays :]
    first, mixed, second = per[:arrays], per[arrays : 2 * arrays], per[2 * arrays : 3 * arrays]
    rest = per[3 * arrays :]
    if z_peers:
        z_out, z_in = rest[:arrays], rest[arrays : 2 * arrays]
        rest = rest[2 * arrays :]
    a_send, a_recv, b_send, b_recv, z_send, z_recv = rest
    me_c, side, over, across, me_f, peers = partners(z_peers)
    greet(side, over, peers)
    f32 = jnp.float32
    started = []

    def go(copy):
        copy.start()
        started.append(copy)

    def slot(s):
        return (me_f + s) % slots if z_peers else s

    far = sorted(range(slots), key=lambda s: -min(s, slots - s))
    order = [(k, s) for k in range(arrays) for s in far]

    def ways(k, s):
        return (side, over) if (k + s) % 2 == 0 else (over, side)

    for k, s in order:
        near, other = ways(k, s)
        go(remote(ins[k].at[slot(s), across], first[k].at[s, 1], a_send.at[1, k, s], a_recv.at[1, k, s], "ctx", near))
        go(remote(ins[k].at[slot(s), near], first[k].at[s, 0], a_send.at[0, k, s], a_recv.at[0, k, s], "ctx", near))

    def middle(k, s):
        near, other = ways(k, s)
        landed = first[k].at[s, 1]
        remote(landed, landed, a_send.at[1, k, s], a_recv.at[1, k, s], "ctx", near).wait_recv()
        mixed[k][s] = (ins[k][slot(s), other].astype(f32) + landed[...].astype(f32)).astype(jnp.bfloat16)
        go(remote(mixed[k].at[s], second[k].at[s], b_send.at[k, s], b_recv.at[k, s], "ctx", other))

    def last(k, s):
        near, other = ways(k, s)
        landed = first[k].at[s, 0]
        remote(landed, landed, a_send.at[0, k, s], a_recv.at[0, k, s], "ctx", near).wait_recv()
        more = second[k].at[s]
        remote(more, more, b_send.at[k, s], b_recv.at[k, s], "ctx", other).wait_recv()
        total = ins[k][slot(s), me_c].astype(f32) + landed[...].astype(f32) + more[...].astype(f32)
        if not z_peers:
            outs[k][s] = total
        elif s == 0:
            outs[k][0] = total
        else:
            z_out[k][s] = total.astype(jnp.bfloat16)
            go(remote(z_out[k].at[s], z_in[k].at[slots - s], z_send.at[k, s], z_recv.at[k, slots - s], "fsdp", peers[s - 1]))

    lag = 3 if len(order) > 4 else len(order)
    for at, (k, s) in enumerate(order):
        middle(k, s)
        if at >= lag:
            last(*order[at - lag])
    for k, s in order[len(order) - lag :]:
        last(k, s)
    if z_peers:
        for k in range(arrays):
            total = outs[k][0]
            for s in range(1, slots):
                ref = z_in[k].at[s]
                remote(ref, ref, z_send.at[k, s], z_recv.at[k, s], "fsdp", peers[0]).wait_recv()
                total = total + ref[...].astype(f32)
            outs[k][0] = total
    for copy in started:
        copy.wait_send()


def scatter_blocks(parts, z_peers, collective_id):
    arrays = len(parts)
    slots = parts[0].shape[0]
    bf16 = jnp.bfloat16
    spec = pl.BlockSpec(memory_space=pltpu.VMEM)
    dims = [x.shape[2:] for x in parts]
    scratch = [pltpu.VMEM((slots, 2) + d, bf16) for d in dims]
    scratch += [pltpu.VMEM((slots,) + d, bf16) for d in dims] * 2
    if z_peers:
        scratch += [pltpu.VMEM((slots,) + d, bf16) for d in dims] * 2
    scratch += [pltpu.SemaphoreType.DMA((2, arrays, slots))] * 2
    scratch += [pltpu.SemaphoreType.DMA((arrays, slots))] * 4
    size = sum(x.size * 2 for x in parts)
    return pl.pallas_call(
        functools.partial(scatter_kernel, arrays, slots, z_peers),
        out_shape=[jax.ShapeDtypeStruct((1 if z_peers else slots,) + d, jnp.float32) for d in dims],
        in_specs=[spec] * arrays,
        out_specs=[spec] * arrays,
        scratch_shapes=scratch,
        compiler_params=pltpu.CompilerParams(
            collective_id=collective_id, has_side_effects=True, vmem_limit_bytes=int(size * 3) + (6 << 20)
        ),
        cost_estimate=pl.CostEstimate(flops=0, bytes_accessed=2 * size, transcendentals=0),
    )(*parts)


def norm_rows(rows_in, row_gain, row_shift):
    centre_mean = jnp.mean(rows_in, axis=-1, keepdims=True)
    centred = rows_in - centre_mean
    variance = jnp.mean(centred * centred, axis=-1, keepdims=True)
    return centred * lax.rsqrt(variance + 1e-05) * row_gain + row_shift


def head_sum(pieces):
    count = lax.axis_size("tp")
    total = pieces
    moved = pieces
    for _ in range(count - 1):
        moved = lax.ppermute(moved, "tp", [(i, (i + 1) % count) for i in range(count)])
        total = total + moved
    return total


def sum_small(arrays):
    sizes = [x.size for x in arrays]
    packed = jnp.concatenate([x.reshape(-1) for x in arrays]).reshape(-1, 128)
    for axis in ("ctx", "fsdp"):
        count = lax.axis_size(axis)
        bit = 1
        while bit < count:
            packed = packed + lax.ppermute(packed, axis, [(i, i ^ bit) for i in range(count)])
            bit *= 2
    flat = packed.reshape(-1)
    result, at = [], 0
    for x, size in zip(arrays, sizes):
        result.append(flat[at : at + size].reshape(x.shape))
        at += size
    return result


def gather_weights(shards):
    if lax.axis_size("fsdp") <= 4:
        full = gather_blocks([x[None] for x in shards], lax.axis_size("fsdp"), True, 1)
        return [x.reshape(-1, x.shape[-1]) for x in full]
    return [lax.all_gather(x, ("fsdp", "ctx"), axis=0, tiled=True) for x in shards]


def scatter_weights(parts):
    slots = lax.axis_size("fsdp")
    if slots <= 4:
        blocks = [x.astype(jnp.bfloat16).reshape(slots, 4, -1, x.shape[-1]) for x in parts]
        return [x[0] for x in scatter_blocks(blocks, True, 2)]
    return [lax.psum_scatter(x, ("fsdp", "ctx"), scatter_dimension=0, tiled=True) for x in parts]


def body(
    layer_input,
    lengths,
    first_gain,
    first_shift,
    qkv_weight,
    qv_bias,
    out_weight,
    out_bias,
    second_gain,
    second_shift,
    up_weight,
    up_bias,
    down_weight,
    down_bias,
    cotangent,
):
    seq_count, span, width = layer_input.shape
    row_count = seq_count * span
    local_width = qkv_weight.shape[2]
    head_count = local_width // HEAD
    full_length = span * lax.axis_size("ctx")
    score_scale = 1.0 / math.sqrt(HEAD)
    f32 = jnp.float32
    bf16 = jnp.bfloat16
    inputs = layer_input.astype(f32).reshape(row_count, width)
    first_shard = jnp.concatenate([qkv_weight[0], qkv_weight[1], qkv_weight[2], out_weight.T], axis=1)
    first_full, up_full, down_full = gather_weights([first_shard, up_weight, down_weight.T])
    qkv_full = first_full[:, : 3 * local_width]
    out_full = first_full[:, 3 * local_width :]
    normed_low = norm_rows(inputs, first_gain, first_shift).astype(bf16)
    projected = jnp.dot(normed_low, qkv_full, preferred_element_type=f32)
    queries = (projected[:, :local_width] + qv_bias[0]).astype(bf16)
    key_local = projected[:, local_width : 2 * local_width].astype(bf16)
    value_local = (projected[:, 2 * local_width :] + qv_bias[1]).astype(bf16)
    key_all, value_all = gather_blocks(
        [x.reshape(seq_count, span, local_width) for x in (key_local, value_local)], seq_count, False, 3
    )
    query_heads = queries.reshape(seq_count, span, head_count, HEAD)
    query_pos = lax.axis_index("ctx") * span + jnp.arange(span, dtype=jnp.int32)
    key_pos = jnp.arange(full_length, dtype=jnp.int32)
    allowed = (key_pos[None, :] <= query_pos[:, None])[None, None] & (
        key_pos[None, None, None, :] < lengths[:, None, None, None]
    )

    def masked_scores(key_source):
        key_heads = key_source.reshape(seq_count, full_length, head_count, HEAD)
        scores = (
            jnp.einsum("suhe,snhe->shun", query_heads, key_heads, preferred_element_type=f32)
            * score_scale
        )
        return jnp.where(allowed, scores, -1e30)

    masked = masked_scores(key_all)
    peak = jnp.max(masked, axis=-1, keepdims=True)
    expo = jnp.where(allowed, jnp.exp(masked - peak), 0.0)
    row_total = jnp.sum(expo, axis=-1, keepdims=True)
    probs = expo / row_total
    probs_low = probs.astype(bf16)
    value_heads = value_all.reshape(seq_count, full_length, head_count, HEAD)
    attended = jnp.einsum("shun,snhe->suhe", probs_low, value_heads, preferred_element_type=f32)
    attended = attended.reshape(row_count, local_width).astype(bf16)
    residual = inputs + head_sum(jnp.einsum("rc,dc->rd", attended, out_full, preferred_element_type=f32)) + out_bias
    normed_two_low = norm_rows(residual, second_gain, second_shift).astype(bf16)
    up_proj = jnp.dot(normed_two_low, up_full, preferred_element_type=f32) + up_bias
    activated_low = jax.nn.gelu(up_proj, approximate=True).astype(bf16)
    mixed = head_sum(jnp.einsum("rf,df->rd", activated_low, down_full, preferred_element_type=f32))
    layer_output = (residual + mixed + down_bias).astype(bf16).reshape(seq_count, span, width)
    grad_out = cotangent.reshape(row_count, width)
    grad_downbias = jnp.sum(grad_out.astype(f32), axis=0)
    grad_downweight = jnp.einsum("rd,rf->df", grad_out, activated_low, preferred_element_type=f32)
    grad_act = jnp.einsum("rd,df->rf", grad_out, down_full, preferred_element_type=f32)
    gelu_back = jax.vjp(lambda z: jax.nn.gelu(z, approximate=True), up_proj)[1]
    grad_up = gelu_back(grad_act)[0].astype(bf16)
    grad_upbias = jnp.sum(grad_up.astype(f32), axis=0)
    grad_upweight = jnp.einsum("rd,rf->df", normed_two_low, grad_up, preferred_element_type=f32)
    grad_normtwo = head_sum(jnp.einsum("rf,df->rd", grad_up, up_full, preferred_element_type=f32))
    second_back = jax.vjp(norm_rows, residual, second_gain, second_shift)[1]
    grad_resid_norm, grad_secondgain, grad_secondshift = second_back(grad_normtwo)
    grad_residual = grad_out.astype(f32) + grad_resid_norm
    grad_branch = grad_residual.astype(bf16)
    grad_outbias = jnp.sum(grad_branch.astype(f32), axis=0)
    grad_outweight = jnp.einsum("rd,rc->dc", grad_branch, attended, preferred_element_type=f32)
    grad_attended = jnp.einsum(
        "rd,dc->rc", grad_branch, out_full, preferred_element_type=f32
    ).astype(bf16)
    probs_again = probs
    probs_low_again = probs_low
    key_heads_back = key_all.reshape(seq_count, full_length, head_count, HEAD)
    value_heads_back = value_all.reshape(seq_count, full_length, head_count, HEAD)
    grad_att_heads = grad_attended.reshape(seq_count, span, head_count, HEAD)
    grad_probs = jnp.einsum(
        "suhe,snhe->shun", grad_att_heads, value_heads_back, preferred_element_type=f32
    )
    inner_total = jnp.sum(probs_again * grad_probs, axis=-1, keepdims=True)
    grad_scores = (probs_again * (grad_probs - inner_total)).astype(bf16)
    grad_query = (
        jnp.einsum("shun,snhe->suhe", grad_scores, key_heads_back, preferred_element_type=f32)
        * score_scale
    )
    grad_query = grad_query.astype(bf16).reshape(row_count, local_width)
    key_part = (
        jnp.einsum("shun,suhe->snhe", grad_scores, query_heads, preferred_element_type=f32)
        * score_scale
    )
    value_part = jnp.einsum(
        "shun,suhe->snhe", probs_low_again, grad_att_heads, preferred_element_type=f32
    )
    key_grads, value_grads = scatter_blocks(
        [x.astype(bf16).reshape(seq_count, 4, span, local_width) for x in (key_part, value_part)], False, 4
    )
    grad_key = key_grads.astype(bf16).reshape(row_count, local_width)
    grad_value = value_grads.astype(bf16).reshape(row_count, local_width)
    grad_proj = jnp.concatenate((grad_query, grad_key, grad_value), axis=1)
    grad_qvbias = jnp.stack(
        (jnp.sum(grad_query.astype(f32), axis=0), jnp.sum(grad_value.astype(f32), axis=0))
    )
    grad_first = jnp.concatenate(
        (jnp.einsum("rd,rc->dc", normed_low, grad_proj, preferred_element_type=f32), grad_outweight), axis=1
    )
    grad_normed = head_sum(jnp.einsum("rc,dc->rd", grad_proj, qkv_full, preferred_element_type=f32))
    first_back = jax.vjp(norm_rows, inputs, first_gain, first_shift)[1]
    grad_in_norm, grad_firstgain, grad_firstshift = first_back(grad_normed)
    grad_input = (grad_residual + grad_in_norm).reshape(seq_count, span, width)
    first_sum, up_sum, down_sum = scatter_weights([grad_first, grad_upweight, grad_downweight])
    weight_grads = (
        jnp.stack([first_sum[:, k * local_width : (k + 1) * local_width] for k in range(3)]),
        first_sum[:, 3 * local_width :].T,
        up_sum,
        down_sum.T,
    )
    small_sums = sum_small(
        (
            grad_firstgain,
            grad_firstshift,
            grad_qvbias,
            grad_outbias,
            grad_secondgain,
            grad_secondshift,
            grad_upbias,
            grad_downbias,
        )
    )
    return (
        layer_output,
        grad_input,
        small_sums[0],
        small_sums[1],
        weight_grads[0],
        small_sums[2],
        weight_grads[1],
        small_sums[3],
        small_sums[4],
        small_sums[5],
        weight_grads[2],
        small_sums[6],
        weight_grads[3],
        small_sums[7],
    )


def solution(mesh):
    in_specs = (
        P("fsdp", "ctx", None),
        P("fsdp"),
        P(),
        P(),
        P(None, ("fsdp", "ctx"), "tp"),
        P(None, "tp"),
        P("tp", ("fsdp", "ctx")),
        P(),
        P(),
        P(),
        P(("fsdp", "ctx"), "tp"),
        P("tp"),
        P("tp", ("fsdp", "ctx")),
        P(),
        P("fsdp", "ctx", None),
    )
    out_specs = (
        P("fsdp", "ctx", None),
        P("fsdp", "ctx", None),
        P(),
        P(),
        P(None, ("fsdp", "ctx"), "tp"),
        P(None, "tp"),
        P("tp", ("fsdp", "ctx")),
        P(),
        P(),
        P(),
        P(("fsdp", "ctx"), "tp"),
        P("tp"),
        P("tp", ("fsdp", "ctx")),
        P(),
    )
    return jax.shard_map(body, mesh=mesh, in_specs=in_specs, out_specs=out_specs, check_vma=False)
```

```python
import functools
import math

import jax
import jax.numpy as jnp
from jax import lax
from jax.experimental import pallas as pl
from jax.experimental.pallas import tpu as pltpu
from jax.sharding import PartitionSpec as P

HEAD = 64
MESH = pl.DeviceIdType.MESH
AHEAD = 3


def partners(z_peers):
    me_c = lax.axis_index("ctx")
    side = me_c + 1 - 2 * (me_c % 2)
    over = (me_c + 2) % 4
    me_f = lax.axis_index("fsdp")
    count = lax.axis_size("fsdp")
    peers = [(me_f + t) % count for t in range(1, count)] if z_peers else []
    return me_c, side, over, 3 - me_c, me_f, peers


def greet(side, over, peers):
    barrier = pltpu.get_barrier_semaphore()
    for target in (side, over):
        pl.semaphore_signal(barrier, inc=1, device_id={"ctx": target}, device_id_type=MESH)
    for target in peers:
        pl.semaphore_signal(barrier, inc=1, device_id={"fsdp": target}, device_id_type=MESH)
    pl.semaphore_wait(barrier, 2 + len(peers))


def remote(src, dst, send, recv, axis, target):
    return pltpu.make_async_remote_copy(
        src_ref=src, dst_ref=dst, send_sem=send, recv_sem=recv,
        device_id={axis: target}, device_id_type=MESH,
    )


def gather_kernel(arrays, slots, z_peers, *refs):
    ins, outs = refs[:arrays], refs[arrays : 2 * arrays]
    z_send, z_recv, xy_send, xy_recv = refs[2 * arrays :]
    me_c, side, over, _, me_f, peers = partners(z_peers)
    greet(side, over, peers)
    started = []

    def go(copy):
        copy.start()
        started.append(copy)

    def slot(s):
        return (me_f + s) % slots if z_peers else s

    def own(k, s):
        if z_peers and s > 0:
            return outs[k].at[slot(s), me_c]
        return ins[k].at[0 if z_peers else s]

    nearest = sorted(range(slots), key=lambda s: min(s, slots - s))
    if z_peers:
        for k in range(arrays):
            for t in nearest[1:]:
                go(remote(ins[k].at[0], outs[k].at[me_f, me_c], z_send.at[k, t], z_recv.at[k, slots - t], "fsdp", peers[t - 1]))
        order = [(k, 0) for k in range(arrays)]
        order += [(k, s) for k in range(arrays) for s in nearest[1:]]
    else:
        order = [(k, s) for k in range(arrays) for s in range(slots)]

    def forward(k, s):
        src = own(k, s)
        if z_peers and s > 0:
            remote(src, src, z_send.at[k, s], z_recv.at[k, s], "fsdp", peers[0]).wait_recv()
        dst = outs[k].at[slot(s), me_c]
        go(remote(src, dst, xy_send.at[0, k, s], xy_recv.at[0, k, s], "ctx", side))
        go(remote(src, dst, xy_send.at[1, k, s], xy_recv.at[1, k, s], "ctx", over))

    def arrived(way, k, s, from_c):
        ref = outs[k].at[slot(s), from_c]
        remote(ref, ref, xy_send.at[way, k, s], xy_recv.at[way, k, s], "ctx", side).wait_recv()
        return ref

    def relay(k, s):
        if (k + s) % 2 == 0:
            ref = arrived(0, k, s, side)
            go(remote(ref, ref, xy_send.at[2, k, s], xy_recv.at[2, k, s], "ctx", over))
        else:
            ref = arrived(1, k, s, over)
            go(remote(ref, ref, xy_send.at[2, k, s], xy_recv.at[2, k, s], "ctx", side))

    lag = 2 if len(order) > 4 else len(order)
    for at, (k, s) in enumerate(order):
        forward(k, s)
        if at >= lag:
            relay(*order[at - lag])
    for k in range(arrays):
        if z_peers:
            outs[k][me_f, me_c] = ins[k][0]
        else:
            for s in range(slots):
                outs[k][s, me_c] = ins[k][s]
    for k, s in order[len(order) - lag :]:
        relay(k, s)
    for k, s in order:
        if (k + s) % 2 == 0:
            arrived(1, k, s, over)
        else:
            arrived(0, k, s, side)
        arrived(2, k, s, 3 - me_c)
    for copy in started:
        copy.wait_send()


def gather_blocks(shards, slots, z_peers, collective_id):
    arrays = len(shards)
    spec = pl.BlockSpec(memory_space=pltpu.VMEM)
    size = sum(x.size * 2 for x in shards) * 4 * (slots if z_peers else 1)
    return pl.pallas_call(
        functools.partial(gather_kernel, arrays, slots, z_peers),
        out_shape=[jax.ShapeDtypeStruct((slots, 4) + x.shape[1:], x.dtype) for x in shards],
        in_specs=[spec] * arrays,
        out_specs=[spec] * arrays,
        scratch_shapes=[
            pltpu.SemaphoreType.DMA((arrays, slots)),
            pltpu.SemaphoreType.DMA((arrays, slots)),
            pltpu.SemaphoreType.DMA((3, arrays, slots)),
            pltpu.SemaphoreType.DMA((3, arrays, slots)),
        ],
        compiler_params=pltpu.CompilerParams(
            collective_id=collective_id, has_side_effects=True, vmem_limit_bytes=int(size * 1.25) + (4 << 20)
        ),
        cost_estimate=pl.CostEstimate(flops=0, bytes_accessed=2 * size, transcendentals=0),
    )(*shards)


def scatter_kernel(arrays, slots, z_peers, *refs):
    ins = refs[:arrays]
    refs = refs[arrays:]
    if z_peers:
        small_in, refs = refs[0], refs[1:]
    outs = refs[:arrays]
    refs = refs[arrays:]
    if z_peers:
        small_out, pair, pair_in, small_all, p_send, p_recv, s_send, s_recv = (refs[0],) + tuple(refs[-7:])
        refs = refs[1:-7]
    per = refs
    first, mixed, second = per[:arrays], per[arrays : 2 * arrays], per[2 * arrays : 3 * arrays]
    rest = per[3 * arrays :]
    if z_peers:
        z_out, z_in = rest[:arrays], rest[arrays : 2 * arrays]
        rest = rest[2 * arrays :]
    a_send, a_recv, b_send, b_recv, z_send, z_recv = rest
    me_c, side, over, across, me_f, peers = partners(z_peers)
    greet(side, over, peers)
    f32 = jnp.float32
    started = []

    def go(copy):
        copy.start()
        started.append(copy)

    def slot(s):
        return (me_f + s) % slots if z_peers else s

    far = sorted(range(slots), key=lambda s: -min(s, slots - s))
    order = [(k, s) for k in range(arrays) for s in far]

    def ways(k, s):
        return (side, over) if (k + s) % 2 == 0 else (over, side)

    def small_pair(stage):
        src = small_in if stage == 0 else pair
        go(remote(src, pair_in.at[stage], p_send.at[stage], p_recv.at[stage], "ctx", (side, over)[stage]))

    def small_add(stage):
        ref = pair_in.at[stage]
        remote(ref, ref, p_send.at[stage], p_recv.at[stage], "ctx", side).wait_recv()
        if stage == 0:
            pair[...] = small_in[...] + ref[...]
            small_pair(1)
        else:
            small_all[me_f] = pair[...] + ref[...]
            for t in range(1, slots):
                go(remote(small_all.at[me_f], small_all.at[me_f], s_send.at[t], s_recv.at[slots - t], "fsdp", peers[t - 1]))

    def small_end():
        for s in range(1, slots):
            ref = small_all.at[slot(s)]
            remote(ref, ref, s_send.at[s], s_recv.at[s], "fsdp", peers[0]).wait_recv()
        total = small_all[0]
        for s in range(1, slots):
            total = total + small_all[s]
        small_out[...] = total

    def first_send(k, s):
        near, other = ways(k, s)
        go(remote(ins[k].at[slot(s), across], first[k].at[s, 1], a_send.at[1, k, s], a_recv.at[1, k, s], "ctx", near))
        go(remote(ins[k].at[slot(s), near], first[k].at[s, 0], a_send.at[0, k, s], a_recv.at[0, k, s], "ctx", near))

    def middle(k, s):
        near, other = ways(k, s)
        landed = first[k].at[s, 1]
        remote(landed, landed, a_send.at[1, k, s], a_recv.at[1, k, s], "ctx", near).wait_recv()
        mixed[k][s] = (ins[k][slot(s), other].astype(f32) + landed[...].astype(f32)).astype(jnp.bfloat16)
        go(remote(mixed[k].at[s], second[k].at[s], b_send.at[k, s], b_recv.at[k, s], "ctx", other))

    def last(k, s):
        near, other = ways(k, s)
        landed = first[k].at[s, 0]
        remote(landed, landed, a_send.at[0, k, s], a_recv.at[0, k, s], "ctx", near).wait_recv()
        more = second[k].at[s]
        remote(more, more, b_send.at[k, s], b_recv.at[k, s], "ctx", other).wait_recv()
        total = ins[k][slot(s), me_c].astype(f32) + landed[...].astype(f32) + more[...].astype(f32)
        if not z_peers:
            outs[k][s] = total
        elif s == 0:
            outs[k][0] = total
        else:
            z_out[k][s] = total.astype(jnp.bfloat16)
            go(remote(z_out[k].at[s], z_in[k].at[slots - s], z_send.at[k, s], z_recv.at[k, slots - s], "fsdp", peers[s - 1]))

    lag = 2 if z_peers else len(order)
    ahead = min(AHEAD, len(order))
    if z_peers:
        small_pair(0)
    for k, s in order[:ahead]:
        first_send(k, s)
    for at, (k, s) in enumerate(order):
        middle(k, s)
        if at + ahead < len(order):
            first_send(*order[at + ahead])
        if z_peers and at in (0, 1):
            small_add(at)
        if at >= lag:
            last(*order[at - lag])
    for k, s in order[len(order) - lag :]:
        last(k, s)
    if z_peers:
        for k in range(arrays):
            total = outs[k][0]
            for s in range(1, slots):
                ref = z_in[k].at[s]
                remote(ref, ref, z_send.at[k, s], z_recv.at[k, s], "fsdp", peers[0]).wait_recv()
                total = total + ref[...].astype(f32)
            outs[k][0] = total
        small_end()
    for copy in started:
        copy.wait_send()


def scatter_blocks(parts, z_peers, collective_id, small=None):
    arrays = len(parts)
    slots = parts[0].shape[0]
    bf16 = jnp.bfloat16
    spec = pl.BlockSpec(memory_space=pltpu.VMEM)
    dims = [x.shape[2:] for x in parts]
    scratch = [pltpu.VMEM((slots, 2) + d, bf16) for d in dims]
    scratch += [pltpu.VMEM((slots,) + d, bf16) for d in dims] * 2
    if z_peers:
        scratch += [pltpu.VMEM((slots,) + d, bf16) for d in dims] * 2
    scratch += [pltpu.SemaphoreType.DMA((2, arrays, slots))] * 2
    scratch += [pltpu.SemaphoreType.DMA((arrays, slots))] * 4
    out_shape = [jax.ShapeDtypeStruct((1 if z_peers else slots,) + d, jnp.float32) for d in dims]
    extra = []
    if z_peers:
        extra = [small]
        out_shape.append(jax.ShapeDtypeStruct(small.shape, small.dtype))
        scratch += [pltpu.VMEM(small.shape, small.dtype), pltpu.VMEM((2,) + small.shape, small.dtype)]
        scratch += [pltpu.VMEM((slots,) + small.shape, small.dtype)]
        scratch += [pltpu.SemaphoreType.DMA((2,))] * 2 + [pltpu.SemaphoreType.DMA((slots,))] * 2
    size = sum(x.size * 2 for x in parts)
    return pl.pallas_call(
        functools.partial(scatter_kernel, arrays, slots, z_peers),
        out_shape=out_shape,
        in_specs=[spec] * (arrays + len(extra)),
        out_specs=[spec] * len(out_shape),
        scratch_shapes=scratch,
        compiler_params=pltpu.CompilerParams(
            collective_id=collective_id, has_side_effects=True, vmem_limit_bytes=int(size * 3) + (6 << 20)
        ),
        cost_estimate=pl.CostEstimate(flops=0, bytes_accessed=2 * size, transcendentals=0),
    )(*parts, *extra)


def norm_rows(rows_in, row_gain, row_shift):
    centre_mean = jnp.mean(rows_in, axis=-1, keepdims=True)
    centred = rows_in - centre_mean
    variance = jnp.mean(centred * centred, axis=-1, keepdims=True)
    return centred * lax.rsqrt(variance + 1e-05) * row_gain + row_shift


def head_sum(pieces):
    count = lax.axis_size("tp")
    total = pieces
    moved = pieces
    for _ in range(count - 1):
        moved = lax.ppermute(moved, "tp", [(i, (i + 1) % count) for i in range(count)])
        total = total + moved
    return total


def pack_small(arrays):
    return jnp.pad(jnp.concatenate([x.reshape(-1) for x in arrays]).reshape(-1, 128), ((0, -sum(x.size for x in arrays) // 128 % 8), (0, 0)))


def unpack_small(packed, arrays):
    flat = packed.reshape(-1)
    result, at = [], 0
    for x in arrays:
        result.append(flat[at : at + x.size].reshape(x.shape))
        at += x.size
    return result


def gather_weights(shards):
    if lax.axis_size("fsdp") <= 4:
        full = gather_blocks([x[None] for x in shards], lax.axis_size("fsdp"), True, 1)
        return [x.reshape(-1, x.shape[-1]) for x in full]
    return [lax.all_gather(x, ("fsdp", "ctx"), axis=0, tiled=True) for x in shards]


def scatter_weights(parts, small):
    slots = lax.axis_size("fsdp")
    if slots <= 4:
        blocks = [x.astype(jnp.bfloat16).reshape(slots, 4, -1, x.shape[-1]) for x in parts]
        *sums, total = scatter_blocks(blocks, True, 2, small)
        return [x[0] for x in sums], total
    sums = [lax.psum_scatter(x, ("fsdp", "ctx"), scatter_dimension=0, tiled=True) for x in parts]
    return sums, lax.psum(small, ("fsdp", "ctx"))


def body(
    layer_input,
    lengths,
    first_gain,
    first_shift,
    qkv_weight,
    qv_bias,
    out_weight,
    out_bias,
    second_gain,
    second_shift,
    up_weight,
    up_bias,
    down_weight,
    down_bias,
    cotangent,
):
    seq_count, span, width = layer_input.shape
    row_count = seq_count * span
    local_width = qkv_weight.shape[2]
    head_count = local_width // HEAD
    full_length = span * lax.axis_size("ctx")
    score_scale = 1.0 / math.sqrt(HEAD)
    f32 = jnp.float32
    bf16 = jnp.bfloat16
    inputs = layer_input.astype(f32).reshape(row_count, width)
    first_shard = jnp.concatenate([qkv_weight[0], qkv_weight[1], qkv_weight[2], out_weight.T], axis=1)
    first_full, up_full, down_full = gather_weights([first_shard, up_weight, down_weight.T])
    qkv_full = first_full[:, : 3 * local_width]
    out_full = first_full[:, 3 * local_width :]
    normed_low = norm_rows(inputs, first_gain, first_shift).astype(bf16)
    projected = jnp.dot(normed_low, qkv_full, preferred_element_type=f32)
    queries = (projected[:, :local_width] + qv_bias[0]).astype(bf16)
    key_local = projected[:, local_width : 2 * local_width].astype(bf16)
    value_local = (projected[:, 2 * local_width :] + qv_bias[1]).astype(bf16)
    key_all, value_all = gather_blocks(
        [x.reshape(seq_count, span, local_width) for x in (key_local, value_local)], seq_count, False, 3
    )
    query_heads = queries.reshape(seq_count, span, head_count, HEAD)
    query_pos = lax.axis_index("ctx") * span + jnp.arange(span, dtype=jnp.int32)
    key_pos = jnp.arange(full_length, dtype=jnp.int32)
    allowed = (key_pos[None, :] <= query_pos[:, None])[None, None] & (
        key_pos[None, None, None, :] < lengths[:, None, None, None]
    )

    def masked_scores(key_source):
        key_heads = key_source.reshape(seq_count, full_length, head_count, HEAD)
        scores = (
            jnp.einsum("suhe,snhe->shun", query_heads, key_heads, preferred_element_type=f32)
            * score_scale
        )
        return jnp.where(allowed, scores, -1e30)

    masked = masked_scores(key_all)
    peak = jnp.max(masked, axis=-1, keepdims=True)
    expo = jnp.where(allowed, jnp.exp(masked - peak), 0.0)
    row_total = jnp.sum(expo, axis=-1, keepdims=True)
    probs = expo / row_total
    probs_low = probs.astype(bf16)
    value_heads = value_all.reshape(seq_count, full_length, head_count, HEAD)
    attended = jnp.einsum("shun,snhe->suhe", probs_low, value_heads, preferred_element_type=f32)
    attended = attended.reshape(row_count, local_width).astype(bf16)
    residual = inputs + head_sum(jnp.einsum("rc,dc->rd", attended, out_full, preferred_element_type=f32)) + out_bias
    normed_two_low = norm_rows(residual, second_gain, second_shift).astype(bf16)
    up_proj = jnp.dot(normed_two_low, up_full, preferred_element_type=f32) + up_bias
    activated_low = jax.nn.gelu(up_proj, approximate=True).astype(bf16)
    mixed = head_sum(jnp.einsum("rf,df->rd", activated_low, down_full, preferred_element_type=f32))
    layer_output = (residual + mixed + down_bias).astype(bf16).reshape(seq_count, span, width)
    grad_out = cotangent.reshape(row_count, width)
    grad_downbias = jnp.sum(grad_out.astype(f32), axis=0)
    grad_downweight = jnp.einsum("rd,rf->df", grad_out, activated_low, preferred_element_type=f32)
    grad_act = jnp.einsum("rd,df->rf", grad_out, down_full, preferred_element_type=f32)
    gelu_back = jax.vjp(lambda z: jax.nn.gelu(z, approximate=True), up_proj)[1]
    grad_up = gelu_back(grad_act)[0].astype(bf16)
    grad_upbias = jnp.sum(grad_up.astype(f32), axis=0)
    grad_upweight = jnp.einsum("rd,rf->df", normed_two_low, grad_up, preferred_element_type=f32)
    grad_normtwo = head_sum(jnp.einsum("rf,df->rd", grad_up, up_full, preferred_element_type=f32))
    second_back = jax.vjp(norm_rows, residual, second_gain, second_shift)[1]
    grad_resid_norm, grad_secondgain, grad_secondshift = second_back(grad_normtwo)
    grad_residual = grad_out.astype(f32) + grad_resid_norm
    grad_branch = grad_residual.astype(bf16)
    grad_outbias = jnp.sum(grad_branch.astype(f32), axis=0)
    grad_outweight = jnp.einsum("rd,rc->dc", grad_branch, attended, preferred_element_type=f32)
    grad_attended = jnp.einsum(
        "rd,dc->rc", grad_branch, out_full, preferred_element_type=f32
    ).astype(bf16)
    probs_again = probs
    probs_low_again = probs_low
    key_heads_back = key_all.reshape(seq_count, full_length, head_count, HEAD)
    value_heads_back = value_all.reshape(seq_count, full_length, head_count, HEAD)
    grad_att_heads = grad_attended.reshape(seq_count, span, head_count, HEAD)
    grad_probs = jnp.einsum(
        "suhe,snhe->shun", grad_att_heads, value_heads_back, preferred_element_type=f32
    )
    inner_total = jnp.sum(probs_again * grad_probs, axis=-1, keepdims=True)
    grad_scores = (probs_again * (grad_probs - inner_total)).astype(bf16)
    grad_query = (
        jnp.einsum("shun,snhe->suhe", grad_scores, key_heads_back, preferred_element_type=f32)
        * score_scale
    )
    grad_query = grad_query.astype(bf16).reshape(row_count, local_width)
    key_part = (
        jnp.einsum("shun,suhe->snhe", grad_scores, query_heads, preferred_element_type=f32)
        * score_scale
    )
    value_part = jnp.einsum(
        "shun,suhe->snhe", probs_low_again, grad_att_heads, preferred_element_type=f32
    )
    key_grads, value_grads = scatter_blocks(
        [x.astype(bf16).reshape(seq_count, 4, span, local_width) for x in (key_part, value_part)], False, 4
    )
    grad_key = key_grads.astype(bf16).reshape(row_count, local_width)
    grad_value = value_grads.astype(bf16).reshape(row_count, local_width)
    grad_proj = jnp.concatenate((grad_query, grad_key, grad_value), axis=1)
    grad_qvbias = jnp.stack(
        (jnp.sum(grad_query.astype(f32), axis=0), jnp.sum(grad_value.astype(f32), axis=0))
    )
    grad_first = jnp.concatenate(
        (jnp.einsum("rd,rc->dc", normed_low, grad_proj, preferred_element_type=f32), grad_outweight), axis=1
    )
    grad_normed = head_sum(jnp.einsum("rc,dc->rd", grad_proj, qkv_full, preferred_element_type=f32))
    first_back = jax.vjp(norm_rows, inputs, first_gain, first_shift)[1]
    grad_in_norm, grad_firstgain, grad_firstshift = first_back(grad_normed)
    grad_input = (grad_residual + grad_in_norm).reshape(seq_count, span, width)
    small_parts = (
        grad_firstgain,
        grad_firstshift,
        grad_qvbias,
        grad_outbias,
        grad_secondgain,
        grad_secondshift,
        grad_upbias,
        grad_downbias,
    )
    (first_sum, up_sum, down_sum), small_total = scatter_weights([grad_first, grad_upweight, grad_downweight], pack_small(small_parts))
    weight_grads = (
        jnp.stack([first_sum[:, k * local_width : (k + 1) * local_width] for k in range(3)]),
        first_sum[:, 3 * local_width :].T,
        up_sum,
        down_sum.T,
    )
    small_sums = unpack_small(small_total, small_parts)
    return (
        layer_output,
        grad_input,
        small_sums[0],
        small_sums[1],
        weight_grads[0],
        small_sums[2],
        weight_grads[1],
        small_sums[3],
        small_sums[4],
        small_sums[5],
        weight_grads[2],
        small_sums[6],
        weight_grads[3],
        small_sums[7],
    )


def solution(mesh):
    in_specs = (
        P("fsdp", "ctx", None),
        P("fsdp"),
        P(),
        P(),
        P(None, ("fsdp", "ctx"), "tp"),
        P(None, "tp"),
        P("tp", ("fsdp", "ctx")),
        P(),
        P(),
        P(),
        P(("fsdp", "ctx"), "tp"),
        P("tp"),
        P("tp", ("fsdp", "ctx")),
        P(),
        P("fsdp", "ctx", None),
    )
    out_specs = (
        P("fsdp", "ctx", None),
        P("fsdp", "ctx", None),
        P(),
        P(),
        P(None, ("fsdp", "ctx"), "tp"),
        P(None, "tp"),
        P("tp", ("fsdp", "ctx")),
        P(),
        P(),
        P(),
        P(("fsdp", "ctx"), "tp"),
        P("tp"),
        P("tp", ("fsdp", "ctx")),
        P(),
    )
    return jax.shard_map(body, mesh=mesh, in_specs=in_specs, out_specs=out_specs, check_vma=False)
```

```python
import functools
import math

import jax
import jax.numpy as jnp
from jax import lax
from jax.experimental import pallas as pl
from jax.experimental.pallas import tpu as pltpu
from jax.sharding import PartitionSpec as P

HEAD = 64
MESH = pl.DeviceIdType.MESH
AHEAD = 3


def partners(z_peers):
    me_c = lax.axis_index("ctx")
    side = me_c + 1 - 2 * (me_c % 2)
    over = (me_c + 2) % 4
    me_f = lax.axis_index("fsdp")
    count = lax.axis_size("fsdp")
    peers = [(me_f + t) % count for t in range(1, count)] if z_peers else []
    return me_c, side, over, 3 - me_c, me_f, peers


def greet(side, over, peers):
    barrier = pltpu.get_barrier_semaphore()
    for target in (side, over):
        pl.semaphore_signal(barrier, inc=1, device_id={"ctx": target}, device_id_type=MESH)
    for target in peers:
        pl.semaphore_signal(barrier, inc=1, device_id={"fsdp": target}, device_id_type=MESH)
    pl.semaphore_wait(barrier, 2 + len(peers))


def remote(src, dst, send, recv, axis, target):
    return pltpu.make_async_remote_copy(
        src_ref=src, dst_ref=dst, send_sem=send, recv_sem=recv,
        device_id={axis: target}, device_id_type=MESH,
    )


def gather_kernel(arrays, slots, z_peers, *refs):
    ins, outs = refs[:arrays], refs[arrays : 2 * arrays]
    z_send, z_recv, xy_send, xy_recv = refs[2 * arrays :]
    me_c, side, over, _, me_f, peers = partners(z_peers)
    greet(side, over, peers)
    started = []

    def go(copy):
        copy.start()
        started.append(copy)

    def slot(s):
        return (me_f + s) % slots if z_peers else s

    def own(k, s):
        if z_peers and s > 0:
            return outs[k].at[slot(s), me_c]
        return ins[k].at[0 if z_peers else s]

    nearest = sorted(range(slots), key=lambda s: min(s, slots - s))
    if z_peers:
        for k in range(arrays):
            for t in nearest[1:]:
                go(remote(ins[k].at[0], outs[k].at[me_f, me_c], z_send.at[k, t], z_recv.at[k, slots - t], "fsdp", peers[t - 1]))
        order = [(k, 0) for k in range(arrays)]
        order += [(k, s) for k in range(arrays) for s in nearest[1:]]
    else:
        order = [(k, s) for k in range(arrays) for s in range(slots)]

    def forward(k, s):
        src = own(k, s)
        if z_peers and s > 0:
            remote(src, src, z_send.at[k, s], z_recv.at[k, s], "fsdp", peers[0]).wait_recv()
        dst = outs[k].at[slot(s), me_c]
        go(remote(src, dst, xy_send.at[0, k, s], xy_recv.at[0, k, s], "ctx", side))
        go(remote(src, dst, xy_send.at[1, k, s], xy_recv.at[1, k, s], "ctx", over))

    def arrived(way, k, s, from_c):
        ref = outs[k].at[slot(s), from_c]
        remote(ref, ref, xy_send.at[way, k, s], xy_recv.at[way, k, s], "ctx", side).wait_recv()
        return ref

    def relay(k, s):
        if (k + s) % 2 == 0:
            ref = arrived(0, k, s, side)
            go(remote(ref, ref, xy_send.at[2, k, s], xy_recv.at[2, k, s], "ctx", over))
        else:
            ref = arrived(1, k, s, over)
            go(remote(ref, ref, xy_send.at[2, k, s], xy_recv.at[2, k, s], "ctx", side))

    lag = 2 if len(order) > 4 else len(order)
    for at, (k, s) in enumerate(order):
        forward(k, s)
        if at >= lag:
            relay(*order[at - lag])
    for k in range(arrays):
        if z_peers:
            outs[k][me_f, me_c] = ins[k][0]
        else:
            for s in range(slots):
                outs[k][s, me_c] = ins[k][s]
    for k, s in order[len(order) - lag :]:
        relay(k, s)
    for k, s in order:
        if (k + s) % 2 == 0:
            arrived(1, k, s, over)
        else:
            arrived(0, k, s, side)
        arrived(2, k, s, 3 - me_c)
    for copy in started:
        copy.wait_send()


def gather_blocks(shards, slots, z_peers, collective_id):
    arrays = len(shards)
    spec = pl.BlockSpec(memory_space=pltpu.VMEM)
    size = sum(x.size * 2 for x in shards) * 4 * (slots if z_peers else 1)
    return pl.pallas_call(
        functools.partial(gather_kernel, arrays, slots, z_peers),
        out_shape=[jax.ShapeDtypeStruct((slots, 4) + x.shape[1:], x.dtype) for x in shards],
        in_specs=[spec] * arrays,
        out_specs=[spec] * arrays,
        scratch_shapes=[
            pltpu.SemaphoreType.DMA((arrays, slots)),
            pltpu.SemaphoreType.DMA((arrays, slots)),
            pltpu.SemaphoreType.DMA((3, arrays, slots)),
            pltpu.SemaphoreType.DMA((3, arrays, slots)),
        ],
        compiler_params=pltpu.CompilerParams(
            collective_id=collective_id, has_side_effects=True, vmem_limit_bytes=int(size * 1.25) + (4 << 20)
        ),
        cost_estimate=pl.CostEstimate(flops=0, bytes_accessed=2 * size, transcendentals=0),
    )(*shards)


def scatter_kernel(arrays, slots, z_peers, *refs):
    ins = refs[:arrays]
    refs = refs[arrays:]
    if z_peers:
        small_in, refs = refs[0], refs[1:]
    outs = refs[:arrays]
    refs = refs[arrays:]
    if z_peers:
        small_out, pair, pair_in, small_all, p_send, p_recv, s_send, s_recv = (refs[0],) + tuple(refs[-7:])
        refs = refs[1:-7]
    per = refs
    first, mixed, second = per[:arrays], per[arrays : 2 * arrays], per[2 * arrays : 3 * arrays]
    rest = per[3 * arrays :]
    if z_peers:
        z_out, z_in = rest[:arrays], rest[arrays : 2 * arrays]
        rest = rest[2 * arrays :]
    a_send, a_recv, b_send, b_recv, z_send, z_recv = rest
    me_c, side, over, across, me_f, peers = partners(z_peers)
    greet(side, over, peers)
    f32 = jnp.float32
    started = []

    def go(copy):
        copy.start()
        started.append(copy)

    def slot(s):
        return (me_f + s) % slots if z_peers else s

    far = sorted(range(slots), key=lambda s: -min(s, slots - s))
    order = [(k, s) for k in range(arrays) for s in far]

    def ways(k, s):
        return (side, over) if (k + s) % 2 == 0 else (over, side)

    def small_pair(stage):
        src = small_in if stage == 0 else pair
        go(remote(src, pair_in.at[stage], p_send.at[stage], p_recv.at[stage], "ctx", (side, over)[stage]))

    def small_add(stage):
        ref = pair_in.at[stage]
        remote(ref, ref, p_send.at[stage], p_recv.at[stage], "ctx", side).wait_recv()
        if stage == 0:
            pair[...] = small_in[...] + ref[...]
            small_pair(1)
        else:
            small_all[me_f] = pair[...] + ref[...]
            for t in range(1, slots):
                go(remote(small_all.at[me_f], small_all.at[me_f], s_send.at[t], s_recv.at[slots - t], "fsdp", peers[t - 1]))

    def small_end():
        for s in range(1, slots):
            ref = small_all.at[slot(s)]
            remote(ref, ref, s_send.at[s], s_recv.at[s], "fsdp", peers[0]).wait_recv()
        total = small_all[0]
        for s in range(1, slots):
            total = total + small_all[s]
        small_out[...] = total

    def first_send(k, s):
        near, other = ways(k, s)
        go(remote(ins[k].at[slot(s), across], first[k].at[s, 1], a_send.at[1, k, s], a_recv.at[1, k, s], "ctx", near))
        go(remote(ins[k].at[slot(s), near], first[k].at[s, 0], a_send.at[0, k, s], a_recv.at[0, k, s], "ctx", near))

    def middle(k, s):
        near, other = ways(k, s)
        landed = first[k].at[s, 1]
        remote(landed, landed, a_send.at[1, k, s], a_recv.at[1, k, s], "ctx", near).wait_recv()
        mixed[k][s] = (ins[k][slot(s), other].astype(f32) + landed[...].astype(f32)).astype(jnp.bfloat16)
        go(remote(mixed[k].at[s], second[k].at[s], b_send.at[k, s], b_recv.at[k, s], "ctx", other))

    def last(k, s):
        near, other = ways(k, s)
        landed = first[k].at[s, 0]
        remote(landed, landed, a_send.at[0, k, s], a_recv.at[0, k, s], "ctx", near).wait_recv()
        more = second[k].at[s]
        remote(more, more, b_send.at[k, s], b_recv.at[k, s], "ctx", other).wait_recv()
        total = ins[k][slot(s), me_c].astype(f32) + landed[...].astype(f32) + more[...].astype(f32)
        if not z_peers:
            outs[k][s] = total
        elif s == 0:
            outs[k][0] = total
        else:
            z_out[k][s] = total.astype(jnp.bfloat16)
            go(remote(z_out[k].at[s], z_in[k].at[slots - s], z_send.at[k, s], z_recv.at[k, slots - s], "fsdp", peers[s - 1]))

    lag = 2 if z_peers else len(order)
    ahead = min(AHEAD, len(order))
    if z_peers:
        small_pair(0)
    for k, s in order[:ahead]:
        first_send(k, s)
    for at, (k, s) in enumerate(order):
        middle(k, s)
        if at + ahead < len(order):
            first_send(*order[at + ahead])
        if z_peers and at in (0, 1):
            small_add(at)
        if at >= lag:
            last(*order[at - lag])
    for k, s in order[len(order) - lag :]:
        last(k, s)
    if z_peers:
        for k in range(arrays):
            total = outs[k][0]
            for s in range(1, slots):
                ref = z_in[k].at[s]
                remote(ref, ref, z_send.at[k, s], z_recv.at[k, s], "fsdp", peers[0]).wait_recv()
                total = total + ref[...].astype(f32)
            outs[k][0] = total
        small_end()
    for copy in started:
        copy.wait_send()


def scatter_blocks(parts, z_peers, collective_id, small=None):
    arrays = len(parts)
    slots = parts[0].shape[0]
    bf16 = jnp.bfloat16
    spec = pl.BlockSpec(memory_space=pltpu.VMEM)
    dims = [x.shape[2:] for x in parts]
    scratch = [pltpu.VMEM((slots, 2) + d, bf16) for d in dims]
    scratch += [pltpu.VMEM((slots,) + d, bf16) for d in dims] * 2
    if z_peers:
        scratch += [pltpu.VMEM((slots,) + d, bf16) for d in dims] * 2
    scratch += [pltpu.SemaphoreType.DMA((2, arrays, slots))] * 2
    scratch += [pltpu.SemaphoreType.DMA((arrays, slots))] * 4
    out_shape = [jax.ShapeDtypeStruct((1 if z_peers else slots,) + d, jnp.float32) for d in dims]
    extra = []
    if z_peers:
        extra = [small]
        out_shape.append(jax.ShapeDtypeStruct(small.shape, small.dtype))
        scratch += [pltpu.VMEM(small.shape, small.dtype), pltpu.VMEM((2,) + small.shape, small.dtype)]
        scratch += [pltpu.VMEM((slots,) + small.shape, small.dtype)]
        scratch += [pltpu.SemaphoreType.DMA((2,))] * 2 + [pltpu.SemaphoreType.DMA((slots,))] * 2
    size = sum(x.size * 2 for x in parts)
    return pl.pallas_call(
        functools.partial(scatter_kernel, arrays, slots, z_peers),
        out_shape=out_shape,
        in_specs=[spec] * (arrays + len(extra)),
        out_specs=[spec] * len(out_shape),
        scratch_shapes=scratch,
        compiler_params=pltpu.CompilerParams(
            collective_id=collective_id, has_side_effects=True, vmem_limit_bytes=int(size * 3) + (6 << 20)
        ),
        cost_estimate=pl.CostEstimate(flops=0, bytes_accessed=2 * size, transcendentals=0),
    )(*parts, *extra)


def norm_rows(rows_in, row_gain, row_shift):
    centre_mean = jnp.mean(rows_in, axis=-1, keepdims=True)
    centred = rows_in - centre_mean
    variance = jnp.mean(centred * centred, axis=-1, keepdims=True)
    return centred * lax.rsqrt(variance + 1e-05) * row_gain + row_shift


def head_sum(pieces):
    count = lax.axis_size("tp")
    total = pieces
    moved = pieces
    for _ in range(count - 1):
        moved = lax.ppermute(moved, "tp", [(i, (i + 1) % count) for i in range(count)])
        total = total + moved
    return total


def pack_small(arrays):
    return jnp.pad(jnp.concatenate([x.reshape(-1) for x in arrays]).reshape(-1, 128), ((0, -sum(x.size for x in arrays) // 128 % 8), (0, 0)))


def unpack_small(packed, arrays):
    flat = packed.reshape(-1)
    result, at = [], 0
    for x in arrays:
        result.append(flat[at : at + x.size].reshape(x.shape))
        at += x.size
    return result


def gather_weights(shards):
    if lax.axis_size("fsdp") <= 4:
        full = gather_blocks([x[None] for x in shards], lax.axis_size("fsdp"), True, 1)
        return [x.reshape(-1, x.shape[-1]) for x in full]
    return [lax.all_gather(x, ("fsdp", "ctx"), axis=0, tiled=True) for x in shards]


def scatter_weights(parts, small):
    slots = lax.axis_size("fsdp")
    if slots <= 4:
        blocks = [x.astype(jnp.bfloat16).reshape(slots, 4, -1, x.shape[-1]) for x in parts]
        *sums, total = scatter_blocks(blocks, True, 2, small)
        return [x[0] for x in sums], total
    sums = [lax.psum_scatter(x, ("fsdp", "ctx"), scatter_dimension=0, tiled=True) for x in parts]
    return sums, lax.psum(small, ("fsdp", "ctx"))


def product(left, right, left_dim, right_dim):
    return lax.dot_general(
        left, right, (((left_dim,), (right_dim,)), ((), ())), preferred_element_type=jnp.float32
    )


def attend_kernel(scale, lengths, q_ref, k_ref, v_ref, probs_ref, out_ref):
    seqs, heads, span, total = probs_ref.shape
    rows = lax.axis_index("ctx") * span + lax.broadcasted_iota(jnp.int32, (span, total), 0)
    keys = lax.broadcasted_iota(jnp.int32, (span, total), 1)
    for s in range(seqs):
        allowed = (keys <= rows) & (keys < lengths[s])
        for h in range(heads):
            at, cols = slice(s * span, (s + 1) * span), slice(h * HEAD, (h + 1) * HEAD)
            scores = product(q_ref[at, cols], k_ref[s, :, cols], 1, 1) * scale
            masked = jnp.where(allowed, scores, -1e30)
            peak = jnp.max(masked, axis=-1, keepdims=True)
            expo = jnp.where(allowed, jnp.exp(masked - peak), 0.0)
            probs = expo / jnp.sum(expo, axis=-1, keepdims=True)
            probs_ref[s, h] = probs
            out_ref[at, cols] = product(probs.astype(jnp.bfloat16), v_ref[s, :, cols], 1, 0).astype(jnp.bfloat16)


def attend_back_kernel(scale, q_ref, k_ref, v_ref, probs_ref, grad_ref, gq_ref, gk_ref, gv_ref):
    seqs, heads, span, _ = probs_ref.shape
    bf16 = jnp.bfloat16
    for s in range(seqs):
        for h in range(heads):
            at, cols = slice(s * span, (s + 1) * span), slice(h * HEAD, (h + 1) * HEAD)
            probs, grad, keys = probs_ref[s, h], grad_ref[at, cols], k_ref[s, :, cols]
            grad_probs = product(grad, v_ref[s, :, cols], 1, 1)
            inner = jnp.sum(probs * grad_probs, axis=-1, keepdims=True)
            grad_scores = (probs * (grad_probs - inner)).astype(bf16)
            gq_ref[at, cols] = (product(grad_scores, keys, 1, 0) * scale).astype(bf16)
            gk_ref[s, :, cols] = (product(grad_scores, q_ref[at, cols], 0, 0) * scale).astype(bf16)
            gv_ref[s, :, cols] = product(probs.astype(bf16), grad, 0, 0).astype(bf16)


def local_call(kernel, outs, args, scalars=0):
    spec = pl.BlockSpec(memory_space=pltpu.VMEM)
    return pl.pallas_call(
        kernel,
        out_shape=[jax.ShapeDtypeStruct(dims, kind) for dims, kind in outs],
        in_specs=[pl.BlockSpec(memory_space=pltpu.SMEM)] * scalars + [spec] * (len(args) - scalars),
        out_specs=[spec] * len(outs),
        compiler_params=pltpu.CompilerParams(vmem_limit_bytes=24 << 20),
    )(*args)


def body(
    layer_input,
    lengths,
    first_gain,
    first_shift,
    qkv_weight,
    qv_bias,
    out_weight,
    out_bias,
    second_gain,
    second_shift,
    up_weight,
    up_bias,
    down_weight,
    down_bias,
    cotangent,
):
    seq_count, span, width = layer_input.shape
    row_count = seq_count * span
    local_width = qkv_weight.shape[2]
    head_count = local_width // HEAD
    full_length = span * lax.axis_size("ctx")
    score_scale = 1.0 / math.sqrt(HEAD)
    f32 = jnp.float32
    bf16 = jnp.bfloat16
    inputs = layer_input.astype(f32).reshape(row_count, width)
    first_shard = jnp.concatenate([qkv_weight[0], qkv_weight[1], qkv_weight[2], out_weight.T], axis=1)
    first_full, up_full, down_full = gather_weights([first_shard, up_weight, down_weight.T])
    qkv_full = first_full[:, : 3 * local_width]
    out_full = first_full[:, 3 * local_width :]
    normed_low = norm_rows(inputs, first_gain, first_shift).astype(bf16)
    projected = jnp.dot(normed_low, qkv_full, preferred_element_type=f32)
    queries = (projected[:, :local_width] + qv_bias[0]).astype(bf16)
    key_local = projected[:, local_width : 2 * local_width].astype(bf16)
    value_local = (projected[:, 2 * local_width :] + qv_bias[1]).astype(bf16)
    key_all, value_all = gather_blocks(
        [x.reshape(seq_count, span, local_width) for x in (key_local, value_local)], seq_count, False, 3
    )
    key_all, value_all = (x.reshape(seq_count, full_length, local_width) for x in (key_all, value_all))
    probs, attended = local_call(
        functools.partial(attend_kernel, score_scale),
        [((seq_count, head_count, span, full_length), f32), ((row_count, local_width), bf16)],
        [lengths, queries, key_all, value_all],
        1,
    )
    residual = inputs + head_sum(jnp.einsum("rc,dc->rd", attended, out_full, preferred_element_type=f32)) + out_bias
    normed_two_low = norm_rows(residual, second_gain, second_shift).astype(bf16)
    up_proj = jnp.dot(normed_two_low, up_full, preferred_element_type=f32) + up_bias
    activated_low = jax.nn.gelu(up_proj, approximate=True).astype(bf16)
    mixed = head_sum(jnp.einsum("rf,df->rd", activated_low, down_full, preferred_element_type=f32))
    layer_output = (residual + mixed + down_bias).astype(bf16).reshape(seq_count, span, width)
    grad_out = cotangent.reshape(row_count, width)
    grad_downbias = jnp.sum(grad_out.astype(f32), axis=0)
    grad_downweight = jnp.einsum("rd,rf->df", grad_out, activated_low, preferred_element_type=f32)
    grad_act = jnp.einsum("rd,df->rf", grad_out, down_full, preferred_element_type=f32)
    gelu_back = jax.vjp(lambda z: jax.nn.gelu(z, approximate=True), up_proj)[1]
    grad_up = gelu_back(grad_act)[0].astype(bf16)
    grad_upbias = jnp.sum(grad_up.astype(f32), axis=0)
    grad_upweight = jnp.einsum("rd,rf->df", normed_two_low, grad_up, preferred_element_type=f32)
    grad_normtwo = head_sum(jnp.einsum("rf,df->rd", grad_up, up_full, preferred_element_type=f32))
    second_back = jax.vjp(norm_rows, residual, second_gain, second_shift)[1]
    grad_resid_norm, grad_secondgain, grad_secondshift = second_back(grad_normtwo)
    grad_residual = grad_out.astype(f32) + grad_resid_norm
    grad_branch = grad_residual.astype(bf16)
    grad_outbias = jnp.sum(grad_branch.astype(f32), axis=0)
    grad_outweight = jnp.einsum("rd,rc->dc", grad_branch, attended, preferred_element_type=f32)
    grad_attended = jnp.einsum(
        "rd,dc->rc", grad_branch, out_full, preferred_element_type=f32
    ).astype(bf16)
    whole = ((seq_count, full_length, local_width), bf16)
    grad_query, key_part, value_part = local_call(
        functools.partial(attend_back_kernel, score_scale),
        [((row_count, local_width), bf16), whole, whole],
        [queries, key_all, value_all, probs, grad_attended],
    )
    key_grads, value_grads = scatter_blocks(
        [x.reshape(seq_count, 4, span, local_width) for x in (key_part, value_part)], False, 4
    )
    grad_key = key_grads.astype(bf16).reshape(row_count, local_width)
    grad_value = value_grads.astype(bf16).reshape(row_count, local_width)
    grad_proj = jnp.concatenate((grad_query, grad_key, grad_value), axis=1)
    grad_qvbias = jnp.stack(
        (jnp.sum(grad_query.astype(f32), axis=0), jnp.sum(grad_value.astype(f32), axis=0))
    )
    grad_first = jnp.concatenate(
        (jnp.einsum("rd,rc->dc", normed_low, grad_proj, preferred_element_type=f32), grad_outweight), axis=1
    )
    grad_normed = head_sum(jnp.einsum("rc,dc->rd", grad_proj, qkv_full, preferred_element_type=f32))
    first_back = jax.vjp(norm_rows, inputs, first_gain, first_shift)[1]
    grad_in_norm, grad_firstgain, grad_firstshift = first_back(grad_normed)
    grad_input = (grad_residual + grad_in_norm).reshape(seq_count, span, width)
    small_parts = (
        grad_firstgain,
        grad_firstshift,
        grad_qvbias,
        grad_outbias,
        grad_secondgain,
        grad_secondshift,
        grad_upbias,
        grad_downbias,
    )
    (first_sum, up_sum, down_sum), small_total = scatter_weights([grad_first, grad_upweight, grad_downweight], pack_small(small_parts))
    weight_grads = (
        jnp.stack([first_sum[:, k * local_width : (k + 1) * local_width] for k in range(3)]),
        first_sum[:, 3 * local_width :].T,
        up_sum,
        down_sum.T,
    )
    small_sums = unpack_small(small_total, small_parts)
    return (
        layer_output,
        grad_input,
        small_sums[0],
        small_sums[1],
        weight_grads[0],
        small_sums[2],
        weight_grads[1],
        small_sums[3],
        small_sums[4],
        small_sums[5],
        weight_grads[2],
        small_sums[6],
        weight_grads[3],
        small_sums[7],
    )


def solution(mesh):
    in_specs = (
        P("fsdp", "ctx", None),
        P("fsdp"),
        P(),
        P(),
        P(None, ("fsdp", "ctx"), "tp"),
        P(None, "tp"),
        P("tp", ("fsdp", "ctx")),
        P(),
        P(),
        P(),
        P(("fsdp", "ctx"), "tp"),
        P("tp"),
        P("tp", ("fsdp", "ctx")),
        P(),
        P("fsdp", "ctx", None),
    )
    out_specs = (
        P("fsdp", "ctx", None),
        P("fsdp", "ctx", None),
        P(),
        P(),
        P(None, ("fsdp", "ctx"), "tp"),
        P(None, "tp"),
        P("tp", ("fsdp", "ctx")),
        P(),
        P(),
        P(),
        P(("fsdp", "ctx"), "tp"),
        P("tp"),
        P("tp", ("fsdp", "ctx")),
        P(),
    )
    return jax.shard_map(body, mesh=mesh, in_specs=in_specs, out_specs=out_specs, check_vma=False)
```
